32 devices in a mesh: ctx: 16 (over z, y, x), tp: 2 (over core).
Axes of the slice: x: 2, y: 2, z: 4, core: 2. Of those that a mesh axis runs over, the one named last changes fastest.
Arguments:
- inputs: bfloat16 [3, 4096, 8192], P(None, 'ctx', 'tp'), may hold values from -6 to 6
- cotangent: bfloat16 [4096, 8192], P('ctx', 'tp'), may hold values from -140 to 140
- short_filter: float32 [3, 7, 8192], P(None, None, 'tp'), may hold values from -2 to 2
- residue: float32 [16, 8192], P(None, 'tp'), may hold values from -0.22 to 0.22
- decay_rate: float32 [16, 8192], P(None, 'tp'), may hold values from 2.4414063e-05 to 0.04
Outputs:
- grad_inputs: bfloat16 [3, 4096, 8192], P(None, 'ctx', 'tp')
- grad_short: float32 [3, 7, 8192], P(None, None, 'tp')
The draws below stay inside these ranges and needn't reach their ends.
All inputs are finite; a program needn't handle non-finite values.
Results may differ from the reference program's by a relative error of at most 0.0057.
Values may be sent and summed in bfloat16 or wider, within the bound.
A program may use at most 320 MiB of HBM per device.

```python
import math
import jax
import jax.numpy as jnp
from jax import lax

C = 8192
SHORT = 7
MODES = 16
SEQ = 4096


def mode_pair(key):
    pick_key = jax.random.fold_in(key, 101)
    residue_key = jax.random.fold_in(key, 202)
    lowest = math.log(0.1 / SEQ)
    highest = math.log(0.04)
    uniform_pick = jax.random.uniform(pick_key, (MODES, C), jnp.float32)
    rates = jnp.exp(lowest + uniform_pick * (highest - lowest))
    normals = jnp.clip(jax.random.normal(residue_key, (MODES, C), jnp.float32), -3.0, 3.0)
    residues = normals * jnp.sqrt(2.0 * rates / MODES)
    return (rates, residues)


def draw_decay_rate(key, part):
    return mode_pair(key)[0]


def draw_residue(key, part):
    return mode_pair(key)[1]


def draw_cotangent(key, part):
    column_key = jax.random.fold_in(key, 7)
    value_key = jax.random.fold_in(key, 8)
    columns = jnp.arange(C, dtype=jnp.float32) / C
    spread = jnp.exp(jax.random.uniform(column_key, (C,), jnp.float32) * math.log(10.0)) * jnp.exp2(columns)
    base_draw = jnp.clip(jax.random.normal(value_key, (SEQ, C), jnp.float32), -4.0, 4.0)
    return (base_draw * spread[None, :]).astype(jnp.bfloat16)


def levels(key, extent, cuts, low, largest):
    def one(dim, shards_of):
        heights = jax.random.uniform(jax.random.fold_in(jax.random.fold_in(key, 6), dim), (shards_of,), jnp.float32, low / len(cuts), largest / len(cuts))
        return jnp.repeat(jnp.exp(heights), extent[dim] // shards_of).reshape((-1,) + (1,) * (len(extent) - dim - 1))

    gain = one(*cuts[0])
    for cut in cuts[1:]:
        gain = gain * one(*cut)
    return gain


def scatter_about(rng, dims, width, bound, pieces=(), held_as=jnp.bfloat16):
    entries = jax.random.normal(rng, dims, jnp.float32) * width
    if len(pieces) > 0:
        entries = levels(rng, dims, pieces, -0.22, 0.18) * entries
    return jnp.clip(entries, min=-bound, max=bound).astype(held_as)


def setup_inputs(seed: int = 0) -> dict:
    seeds = jax.random.split(jax.random.key(seed), 6)
    inputs = scatter_about(seeds[0], (3, SEQ, C), 1.0, 6.0, ((1, 16), (2, 2)))
    cotangent = draw_cotangent(jax.random.fold_in(seeds[5], 71), 0)
    short_filter = scatter_about(seeds[2], (3, SHORT, C), SHORT ** -0.5, 2.0, ((2, 2),), jnp.float32)
    residue = draw_residue(jax.random.fold_in(seeds[5], 71), 0)
    decay_rate = draw_decay_rate(jax.random.fold_in(seeds[5], 71), 0)
    return dict(inputs=inputs, cotangent=cotangent, short_filter=short_filter, residue=residue, decay_rate=decay_rate)


def reference(inputs, cotangent, short_filter, residue, decay_rate):
    block_width = math.gcd(C, 256)
    block_starts = jnp.arange(C // block_width, dtype=jnp.int32) * block_width
    frame_len = 2 * SEQ
    offsets = jnp.arange(SEQ, dtype=jnp.float32)

    def one_block(first_chan):
        input_block = lax.dynamic_slice_in_dim(inputs, first_chan, block_width, 2).astype(jnp.float32)
        weights = lax.dynamic_slice_in_dim(short_filter, first_chan, block_width, 2)
        residue_part = lax.dynamic_slice_in_dim(residue, first_chan, block_width, 1)
        rate_part = lax.dynamic_slice_in_dim(decay_rate, first_chan, block_width, 1)
        grad_out = lax.dynamic_slice_in_dim(cotangent, first_chan, block_width, 1).astype(jnp.float32)
        padded = jnp.pad(input_block, ((0, 0), (SHORT - 1, 0), (0, 0)))
        mixed_all = jnp.zeros((3, SEQ, block_width), jnp.float32)
        for offset in range(SHORT):
            mixed_all = mixed_all + weights[:, offset, None, :] * padded[:, SHORT - 1 - offset:SHORT - 1 - offset + SEQ, :]
        gated_kv = lax.optimization_barrier((mixed_all[1] * mixed_all[2]).astype(jnp.bfloat16))
        gated_wide = gated_kv.astype(jnp.float32)
        grad_mixer = lax.optimization_barrier((grad_out * mixed_all[0]).astype(jnp.bfloat16))
        grad_wide = grad_mixer.astype(jnp.float32)
        long_filter = jnp.zeros((SEQ, block_width), jnp.float32)
        for mode_index in range(MODES):
            long_filter = long_filter + residue_part[mode_index][None, :] * jnp.exp(-rate_part[mode_index][None, :] * offsets[:, None])
        filter_spec = jnp.fft.rfft(long_filter, n=frame_len, axis=0)
        gated_spec = jnp.fft.rfft(gated_wide, n=frame_len, axis=0)
        grad_spec = jnp.fft.rfft(grad_wide, n=frame_len, axis=0)
        mixer = jnp.fft.irfft(gated_spec * filter_spec, n=frame_len, axis=0)[:SEQ]
        grad_gated = jnp.fft.irfft(jnp.conj(filter_spec) * grad_spec, n=frame_len, axis=0)[:SEQ]
        grad_query = grad_out * mixer
        grad_key = grad_gated * mixed_all[2]
        grad_value = grad_gated * mixed_all[1]
        grad_mix = lax.optimization_barrier(jnp.stack([grad_query, grad_key, grad_value]).astype(jnp.bfloat16))
        grad_mix_wide = grad_mix.astype(jnp.float32)
        grad_padded = jnp.pad(grad_mix_wide, ((0, 0), (0, SHORT - 1), (0, 0)))
        grad_in = jnp.zeros((3, SEQ, block_width), jnp.float32)
        for offset in range(SHORT):
            grad_in = grad_in + weights[:, offset, None, :] * grad_padded[:, offset:offset + SEQ, :]
        short_grad = jnp.stack([lax.optimization_barrier(jnp.sum(grad_mix_wide * padded[:, SHORT - 1 - offset:SHORT - 1 - offset + SEQ, :], axis=1)) for offset in range(SHORT)], axis=1)
        return (grad_in.astype(jnp.bfloat16), short_grad)
    results = lax.map(one_block, block_starts)
    grad_inputs = jnp.moveaxis(results[0], 0, 2).reshape(3, SEQ, C)
    short_grad = jnp.moveaxis(results[1], 0, 2).reshape(3, SHORT, C)
    squares = jnp.sum(short_grad * short_grad)
    clip_limit = math.sqrt(3 * C * SHORT)
    factor = jnp.minimum(1.0, clip_limit / (jnp.sqrt(squares) + 1e-06))
    return (grad_inputs, short_grad * factor)
```

```python
import math

import jax
import jax.numpy as jnp
import numpy as np
from jax import lax
from jax.experimental import pallas as pl
from jax.experimental.pallas import tpu as pltpu
from jax.sharding import PartitionSpec as P

LANES = 128
RIM = 8
VMEM_LIMIT = 48 * 1024 * 1024


def passed_along(shard, axis, by):
    length = lax.axis_size(axis)
    pairs = [(i, i + by) for i in range(length) if 0 <= i + by < length]
    return lax.ppermute(shard, axis, pairs)


def spectral_table(rows):
    frame = 2 * rows
    freq = np.arange(rows)[:, None]
    pos = np.arange(rows)[None, :]
    angles = (freq * pos % frame) * (2.0 * math.pi / frame)
    lower = -np.sin(angles)
    lower[0] = 1.0 - 2.0 * (np.arange(rows) % 2)
    return np.concatenate([np.cos(angles), lower], axis=0).astype(np.float32)


def split_table(table):
    high = table.astype(jnp.bfloat16)
    low = (table - high.astype(np.float32)).astype(jnp.bfloat16)
    return high, low


def mm(a, b):
    return jnp.dot(a, b, preferred_element_type=jnp.float32)


def row_ids():
    return lax.broadcasted_iota(jnp.int32, (8, LANES), 0).astype(jnp.float32)


def filter_kernel(res_ref, rate_ref, high_ref, low_ref, spec_ref, taps):
    modes, width = res_ref.shape
    rows = taps.shape[0]
    ids = row_ids()

    @pl.loop(0, width // LANES)
    def _(chunk):
        lanes = pl.ds(pl.multiple_of(chunk * LANES, LANES), LANES)
        terms = []
        steps = []
        for n in range(modes):
            rate = jnp.broadcast_to(rate_ref[n : n + 1, lanes], (8, LANES))
            terms.append(res_ref[n : n + 1, lanes] * jnp.exp(-rate * ids))
            steps.append(jnp.exp(-8.0 * rate))

        def body(block, terms):
            total = list(terms)
            while len(total) > 1:
                total = [total[i] + total[i + 1] for i in range(0, len(total) - 1, 2)] + (
                    [total[-1]] if len(total) % 2 else []
                )
            taps[pl.ds(pl.multiple_of(block * 8, 8), 8), lanes] = total[0]
            return tuple(t * s for t, s in zip(terms, steps))

        lax.fori_loop(0, rows // 8, body, tuple(terms), unroll=4)

    whole = taps[...]
    main = whole.astype(jnp.bfloat16)
    rest = (whole - main.astype(jnp.float32)).astype(jnp.bfloat16)
    spec = mm(high_ref[...], main) + (mm(low_ref[...], main) + mm(high_ref[...], rest))
    index = lax.broadcasted_iota(jnp.int32, spec.shape, 0)
    edge = jnp.logical_or(index == 0, index == rows)
    spec_ref[...] = spec * jnp.where(edge, 0.5 / rows, 1.0 / rows)


def fill_extended(ext, in_ref, rim_ref, lanes):
    rows = in_ref.shape[1]
    for i in range(3):
        ext[i, 0:RIM, :] = rim_ref[i, :, lanes]
        ext[i, RIM : RIM + rows, :] = in_ref[i, :, lanes].astype(jnp.float32)


def mix_kernel(
    in_ref, rim_ref, cot_ref, short_ref, rate_ref,
    gated_ref, grad_ref, key_ref, value_ref, state_ref, ext, rowed,
):
    rows, width = cot_ref.shape
    modes = rate_ref.shape[0]
    taps = short_ref.shape[1]
    part = 32
    ids = row_ids()

    @pl.loop(0, width // LANES)
    def _(chunk):
        lanes = pl.ds(pl.multiple_of(chunk * LANES, LANES), LANES)
        fill_extended(ext, in_ref, rim_ref, lanes)
        for first in range(0, rows, part):
            mixed = []
            for i in range(3):
                total = None
                for j in range(taps):
                    term = short_ref[i, j : j + 1, lanes] * ext[i, first + RIM - j : first + RIM - j + part, :]
                    total = term if total is None else total + term
                mixed.append(total)
            here = slice(first, first + part)
            gated_ref[here, lanes] = (mixed[1] * mixed[2]).astype(jnp.bfloat16)
            grad_ref[here, lanes] = (cot_ref[here, lanes].astype(jnp.float32) * mixed[0]).astype(jnp.bfloat16)
            key_ref[here, lanes] = mixed[1].astype(jnp.bfloat16)
            value_ref[here, lanes] = mixed[2].astype(jnp.bfloat16)

        steps = [
            jnp.exp(-8.0 * jnp.broadcast_to(rate_ref[n : n + 1, lanes], (8, LANES)))
            for n in range(modes)
        ]

        def body(block, carry):
            ends, starts = carry
            up = pl.multiple_of(block * 16, 16)
            down = pl.multiple_of(rows - 16 - block * 16, 16)
            ahead = gated_ref[pl.ds(up, 16), lanes].astype(jnp.float32)
            behind = grad_ref[pl.ds(down, 16), lanes].astype(jnp.float32)
            ends = [e * s + ahead[0:8] for e, s in zip(ends, steps)]
            starts = [e * s + behind[8:16] for e, s in zip(starts, steps)]
            ends = [e * s + ahead[8:16] for e, s in zip(ends, steps)]
            starts = [e * s + behind[0:8] for e, s in zip(starts, steps)]
            return tuple(ends), tuple(starts)

        zero = tuple(jnp.zeros((8, LANES), jnp.float32) for _ in range(modes))
        ends, starts = lax.fori_loop(0, rows // 16, body, (zero, zero), unroll=2)
        for n in range(modes):
            rate = jnp.broadcast_to(rate_ref[n : n + 1, lanes], (8, LANES))
            rowed[n : n + 1, :] = jnp.sum(ends[n] * jnp.exp(-rate * (7.0 - ids)), axis=0, keepdims=True)
            rowed[modes + n : modes + n + 1, :] = jnp.sum(
                starts[n] * jnp.exp(-rate * ids), axis=0, keepdims=True
            )
        state_ref[0, :, lanes] = rowed[0:modes, :].astype(jnp.bfloat16)
        state_ref[1, :, lanes] = rowed[modes : 2 * modes, :].astype(jnp.bfloat16)


def local_kernel(gated_ref, grad_ref, spec_ref, high_ref, low_ref, hight_ref, lowt_ref, fwd_ref, back_ref):
    rows = gated_ref.shape[0]
    real = spec_ref[0:rows, :]
    lower = spec_ref[rows : 2 * rows, :]
    first = lax.broadcasted_iota(jnp.int32, real.shape, 0) == 0
    imag = jnp.where(first, 0.0, lower)
    other = jnp.where(first, lower, real)

    def convolved(signal, sign, out_ref):
        seen = mm(high_ref[...], signal) + mm(low_ref[...], signal)
        a = seen[0:rows, :]
        b = seen[rows : 2 * rows, :]
        imag_s = imag * sign
        top = (a * real - b * imag_s).astype(jnp.bfloat16)
        bottom = (a * imag_s + b * other).astype(jnp.bfloat16)
        both = jnp.concatenate([top, bottom], axis=0)
        out_ref[...] = mm(hight_ref[...], both) + mm(lowt_ref[...], both)

    convolved(gated_ref[...], 1.0, fwd_ref)
    convolved(grad_ref[...], -1.0, back_ref)


def scan_kernel(states_ref, step_ref, out_ref):
    count = states_ref.shape[0]
    step = step_ref[...]
    zero = jnp.zeros(step.shape, jnp.float32)

    def up(j, carry):
        out_ref[j, 0, :, :] = carry.astype(jnp.bfloat16)
        return carry * step + states_ref[j, 0, :, :].astype(jnp.float32)

    lax.fori_loop(0, count, up, zero)

    def down(i, carry):
        j = count - 1 - i
        out_ref[j, 1, :, :] = carry.astype(jnp.bfloat16)
        return carry * step + states_ref[j, 1, :, :].astype(jnp.float32)

    lax.fori_loop(0, count, down, zero)


def apply_kernel(
    bound_ref, res_ref, rate_ref, fwd_ref, back_ref, key_ref, value_ref, cot_ref, in_ref, rim_ref,
    gm_ref, short_ref, ext, far,
):
    rows, width = cot_ref.shape
    modes = rate_ref.shape[0]
    taps = short_ref.shape[1]
    part = 32
    ids = row_ids()

    @pl.loop(0, width // LANES)
    def _(chunk):
        lanes = pl.ds(pl.multiple_of(chunk * LANES, LANES), LANES)
        fill_extended(ext, in_ref, rim_ref, lanes)
        before = bound_ref[0, :, lanes].astype(jnp.float32) * res_ref[:, lanes]
        after = bound_ref[1, :, lanes].astype(jnp.float32) * res_ref[:, lanes]
        ups = []
        downs = []
        steps = []
        for n in range(modes):
            rate = jnp.broadcast_to(rate_ref[n : n + 1, lanes], (8, LANES))
            ups.append(before[n : n + 1, :] * jnp.exp(-rate * (ids + 1.0)))
            downs.append(after[n : n + 1, :] * jnp.exp(-rate * (8.0 - ids)))
            steps.append(jnp.exp(-8.0 * rate))

        def summed(terms):
            total = list(terms)
            while len(total) > 1:
                total = [total[i] + total[i + 1] for i in range(0, len(total) - 1, 2)] + (
                    [total[-1]] if len(total) % 2 else []
                )
            return total[0]

        def body(block, carry):
            ups, downs = carry
            up = pl.ds(pl.multiple_of(block * 8, 8), 8)
            down = pl.ds(pl.multiple_of(rows - 8 - block * 8, 8), 8)
            far[0, up, :] = fwd_ref[up, lanes] + summed(ups)
            far[1, down, :] = back_ref[down, lanes] + summed(downs)
            return (
                tuple(t * s for t, s in zip(ups, steps)),
                tuple(t * s for t, s in zip(downs, steps)),
            )

        lax.fori_loop(0, rows // 8, body, (tuple(ups), tuple(downs)), unroll=2)

        sums = [[None] * taps for _ in range(3)]
        for first in range(0, rows, part):
            here = slice(first, first + part)
            mixer = far[0, here, :]
            back = far[1, here, :]
            grads = (
                cot_ref[here, lanes].astype(jnp.float32) * mixer,
                back * value_ref[here, lanes].astype(jnp.float32),
                back * key_ref[here, lanes].astype(jnp.float32),
            )
            for i in range(3):
                kept = grads[i].astype(jnp.bfloat16)
                gm_ref[i, here, lanes] = kept
                wide = kept.astype(jnp.float32)
                for j in range(taps):
                    term = wide * ext[i, first + RIM - j : first + RIM - j + part, :]
                    folded = jnp.sum(term.reshape(part // 8, 8, LANES), axis=0)
                    sums[i][j] = folded if sums[i][j] is None else sums[i][j] + folded
        for i in range(3):
            for j in range(taps):
                short_ref[i, j : j + 1, lanes] = jnp.sum(sums[i][j], axis=0, keepdims=True)


def spread_kernel(gm_ref, rim_ref, short_ref, out_ref, ext):
    rows, width = gm_ref.shape[1:]
    taps = short_ref.shape[1]
    part = 32

    @pl.loop(0, width // LANES)
    def _(chunk):
        lanes = pl.ds(pl.multiple_of(chunk * LANES, LANES), LANES)
        for i in range(3):
            ext[i, 0:rows, :] = gm_ref[i, :, lanes].astype(jnp.float32)
            ext[i, rows : rows + RIM, :] = rim_ref[i, :, lanes]
        for first in range(0, rows, part):
            for i in range(3):
                total = None
                for j in range(taps):
                    term = short_ref[i, j : j + 1, lanes] * ext[i, first + j : first + j + part, :]
                    total = term if total is None else total + term
                out_ref[i, first : first + part, lanes] = total.astype(jnp.bfloat16)


def tiled(shape, tile):
    lead = len(shape) - 1
    return pl.BlockSpec(tuple(shape[:-1]) + (tile,), lambda c: (0,) * lead + (c,))


def fixed(shape):
    return pl.BlockSpec(tuple(shape), lambda c: (0,) * len(shape))


def over_channels(kernel, operands, tables, outs, scratch, tile, flops):
    channels = operands[0].shape[-1]
    total_bytes = sum(a.size * a.dtype.itemsize for a in operands + tables)
    total_bytes += sum(math.prod(o.shape) * o.dtype.itemsize for o in outs)
    return pl.pallas_call(
        kernel,
        grid=(channels // tile,),
        in_specs=[tiled(a.shape, tile) for a in operands] + [fixed(a.shape) for a in tables],
        out_specs=[tiled(o.shape, tile) for o in outs],
        out_shape=outs,
        scratch_shapes=scratch,
        compiler_params=pltpu.CompilerParams(vmem_limit_bytes=VMEM_LIMIT),
        cost_estimate=pl.CostEstimate(flops=flops, bytes_accessed=total_bytes, transcendentals=0),
    )(*operands, *tables)


def per_device(inputs, cotangent, short_filter, residue, decay_rate):
    rows, channels = cotangent.shape
    modes = residue.shape[0]
    taps = short_filter.shape[1]
    ctx_count = lax.axis_size("ctx")
    narrow = channels // ctx_count
    tile = math.gcd(channels, 512)
    f32 = jnp.float32
    bf16 = jnp.bfloat16
    shape = jax.ShapeDtypeStruct
    high, low = split_table(spectral_table(rows))
    tables = [jnp.asarray(high), jnp.asarray(low)]
    turned = [jnp.asarray(np.ascontiguousarray(high.T)), jnp.asarray(np.ascontiguousarray(low.T))]
    ext_rows = pltpu.VMEM((3, rows + RIM, LANES), f32)

    rim = passed_along(inputs[:, rows - RIM :, :], "ctx", 1).astype(f32)
    (spec,) = over_channels(
        filter_kernel, [residue, decay_rate], tables,
        [shape((2 * rows, channels), f32)], [pltpu.VMEM((rows, tile), f32)], tile,
        6 * 2 * rows * rows * channels,
    )
    gated, grad_mixer, key_mix, value_mix, states = over_channels(
        mix_kernel, [inputs, rim, cotangent, short_filter, decay_rate], [],
        [shape((rows, channels), bf16)] * 4 + [shape((2, modes, channels), bf16)],
        [ext_rows, pltpu.VMEM((2 * modes, LANES), f32)], tile, 110 * rows * channels,
    )
    sent = states.reshape(2, modes, ctx_count, narrow).transpose(2, 0, 1, 3)
    arrived = lax.all_to_all(sent, "ctx", split_axis=0, concat_axis=0, tiled=True)
    fwd_part, back_part = over_channels(
        local_kernel, [gated, grad_mixer, spec], tables + turned,
        [shape((rows, channels), f32)] * 2, [], tile, 16 * 2 * rows * rows * channels,
    )
    first_chan = lax.axis_index("ctx") * narrow
    rate_part = lax.dynamic_slice_in_dim(decay_rate, first_chan, narrow, 1)
    bounds = pl.pallas_call(
        scan_kernel,
        out_shape=shape(arrived.shape, bf16),
        compiler_params=pltpu.CompilerParams(vmem_limit_bytes=VMEM_LIMIT),
    )(arrived, jnp.exp(-rate_part * rows))
    returned = lax.all_to_all(bounds, "ctx", split_axis=0, concat_axis=0, tiled=True)
    bound = returned.transpose(1, 2, 0, 3).reshape(2, modes, channels)
    grad_mix, short_grad = over_channels(
        apply_kernel,
        [bound, residue, decay_rate, fwd_part, back_part, key_mix, value_mix, cotangent, inputs, rim],
        [],
        [shape((3, rows, channels), bf16), shape((3, taps, channels), f32)],
        [ext_rows, pltpu.VMEM((2, rows, LANES), f32)], tile, 110 * rows * channels,
    )
    next_rim = passed_along(grad_mix[:, :RIM, :], "ctx", -1).astype(f32)
    short_sum = lax.psum(short_grad, "ctx")
    (grad_inputs,) = over_channels(
        spread_kernel, [grad_mix, next_rim, short_filter], [],
        [shape((3, rows, channels), bf16)], [ext_rows], tile, 42 * rows * channels,
    )
    squares = lax.psum(jnp.sum(short_sum * short_sum), "tp")
    clip_limit = math.sqrt(3 * channels * lax.axis_size("tp") * taps)
    factor = jnp.minimum(1.0, clip_limit / (jnp.sqrt(squares) + 1e-06))
    return (grad_inputs, short_sum * factor)


def solution(mesh):
    return jax.shard_map(
        per_device,
        mesh=mesh,
        in_specs=(
            P(None, "ctx", "tp"),
            P("ctx", "tp"),
            P(None, None, "tp"),
            P(None, "tp"),
            P(None, "tp"),
        ),
        out_specs=(P(None, "ctx", "tp"), P(None, None, "tp")),
        check_vma=False,
    )
```

```python
import math

import jax
import jax.numpy as jnp
import numpy as np
from jax import lax
from jax.experimental import pallas as pl
from jax.experimental.pallas import tpu as pltpu
from jax.sharding import PartitionSpec as P

LANES = 128
RIM = 8
VMEM_LIMIT = 60 * 1024 * 1024


def passed_along(shard, axis, by):
    length = lax.axis_size(axis)
    pairs = [(i, i + by) for i in range(length) if 0 <= i + by < length]
    return lax.ppermute(shard, axis, pairs)


def spectral_table(rows):
    frame = 2 * rows
    freq = np.arange(rows)[:, None]
    pos = np.arange(rows)[None, :]
    angles = (freq * pos % frame) * (2.0 * math.pi / frame)
    lower = -np.sin(angles)
    lower[0] = 1.0 - 2.0 * (np.arange(rows) % 2)
    return np.concatenate([np.cos(angles), lower], axis=0).astype(np.float32)


def split_table(table):
    high = table.astype(jnp.bfloat16)
    low = (table - high.astype(np.float32)).astype(jnp.bfloat16)
    return high, low


def mm(a, b):
    return jnp.dot(a, b, preferred_element_type=jnp.float32)


def row_ids():
    return lax.broadcasted_iota(jnp.int32, (8, LANES), 0).astype(jnp.float32)


def filter_kernel(res_ref, rate_ref, high_ref, low_ref, spec_ref, taps):
    modes, width = res_ref.shape
    rows = taps.shape[0]
    ids = row_ids()

    @pl.loop(0, width // LANES)
    def _(chunk):
        lanes = pl.ds(pl.multiple_of(chunk * LANES, LANES), LANES)
        terms = []
        steps = []
        for n in range(modes):
            rate = jnp.broadcast_to(rate_ref[n : n + 1, lanes], (8, LANES))
            terms.append(res_ref[n : n + 1, lanes] * jnp.exp(-rate * ids))
            steps.append(jnp.exp(-8.0 * rate))

        def body(block, terms):
            total = list(terms)
            while len(total) > 1:
                total = [total[i] + total[i + 1] for i in range(0, len(total) - 1, 2)] + (
                    [total[-1]] if len(total) % 2 else []
                )
            taps[pl.ds(pl.multiple_of(block * 8, 8), 8), lanes] = total[0]
            return tuple(t * s for t, s in zip(terms, steps))

        lax.fori_loop(0, rows // 8, body, tuple(terms), unroll=4)

    whole = taps[...]
    main = whole.astype(jnp.bfloat16)
    rest = (whole - main.astype(jnp.float32)).astype(jnp.bfloat16)
    spec = mm(high_ref[...], main) + (mm(low_ref[...], main) + mm(high_ref[...], rest))
    index = lax.broadcasted_iota(jnp.int32, spec.shape, 0)
    edge = jnp.logical_or(index == 0, index == rows)
    spec_ref[...] = spec * jnp.where(edge, 0.5 / rows, 1.0 / rows)


def fill_extended(ext, in_ref, rim_ref, lanes):
    rows = in_ref.shape[1]
    for i in range(3):
        ext[i, 0:RIM, :] = rim_ref[i, :, lanes]
        ext[i, RIM : RIM + rows, :] = in_ref[i, :, lanes].astype(jnp.float32)


def mix_kernel(
    in_ref, rim_ref, cot_ref, short_ref, rate_ref,
    gated_ref, grad_ref, key_ref, value_ref, state_ref, ext, rowed,
):
    rows, width = cot_ref.shape
    modes = rate_ref.shape[0]
    taps = short_ref.shape[1]
    part = 32
    ids = row_ids()

    @pl.loop(0, width // LANES)
    def _(chunk):
        lanes = pl.ds(pl.multiple_of(chunk * LANES, LANES), LANES)
        fill_extended(ext, in_ref, rim_ref, lanes)
        for first in range(0, rows, part):
            mixed = []
            for i in range(3):
                total = None
                for j in range(taps):
                    term = short_ref[i, j : j + 1, lanes] * ext[i, first + RIM - j : first + RIM - j + part, :]
                    total = term if total is None else total + term
                mixed.append(total)
            here = slice(first, first + part)
            gated_ref[here, lanes] = (mixed[1] * mixed[2]).astype(jnp.bfloat16)
            grad_ref[here, lanes] = (cot_ref[here, lanes].astype(jnp.float32) * mixed[0]).astype(jnp.bfloat16)
            key_ref[here, lanes] = mixed[1].astype(jnp.bfloat16)
            value_ref[here, lanes] = mixed[2].astype(jnp.bfloat16)

        steps = [
            jnp.exp(-8.0 * jnp.broadcast_to(rate_ref[n : n + 1, lanes], (8, LANES)))
            for n in range(modes)
        ]

        def body(block, carry):
            ends, starts = carry
            up = pl.multiple_of(block * 16, 16)
            down = pl.multiple_of(rows - 16 - block * 16, 16)
            ahead = gated_ref[pl.ds(up, 16), lanes].astype(jnp.float32)
            behind = grad_ref[pl.ds(down, 16), lanes].astype(jnp.float32)
            ends = [e * s + ahead[0:8] for e, s in zip(ends, steps)]
            starts = [e * s + behind[8:16] for e, s in zip(starts, steps)]
            ends = [e * s + ahead[8:16] for e, s in zip(ends, steps)]
            starts = [e * s + behind[0:8] for e, s in zip(starts, steps)]
            return tuple(ends), tuple(starts)

        zero = tuple(jnp.zeros((8, LANES), jnp.float32) for _ in range(modes))
        ends, starts = lax.fori_loop(0, rows // 16, body, (zero, zero), unroll=2)
        for n in range(modes):
            rate = jnp.broadcast_to(rate_ref[n : n + 1, lanes], (8, LANES))
            rowed[n : n + 1, :] = jnp.sum(ends[n] * jnp.exp(-rate * (7.0 - ids)), axis=0, keepdims=True)
            rowed[modes + n : modes + n + 1, :] = jnp.sum(
                starts[n] * jnp.exp(-rate * ids), axis=0, keepdims=True
            )
        state_ref[0, :, lanes] = rowed[0:modes, :].astype(jnp.bfloat16)
        state_ref[1, :, lanes] = rowed[modes : 2 * modes, :].astype(jnp.bfloat16)


def local_kernel(gated_ref, grad_ref, spec_ref, high_ref, low_ref, hight_ref, lowt_ref, fwd_ref, back_ref):
    rows = gated_ref.shape[0]
    real = spec_ref[0:rows, :]
    lower = spec_ref[rows : 2 * rows, :]
    first = lax.broadcasted_iota(jnp.int32, real.shape, 0) == 0
    imag = jnp.where(first, 0.0, lower)
    other = jnp.where(first, lower, real)

    def convolved(signal, sign, out_ref):
        seen = mm(high_ref[...], signal) + mm(low_ref[...], signal)
        a = seen[0:rows, :]
        b = seen[rows : 2 * rows, :]
        imag_s = imag * sign
        top = (a * real - b * imag_s).astype(jnp.bfloat16)
        bottom = (a * imag_s + b * other).astype(jnp.bfloat16)
        both = jnp.concatenate([top, bottom], axis=0)
        out_ref[...] = mm(hight_ref[...], both) + mm(lowt_ref[...], both)

    convolved(gated_ref[...], 1.0, fwd_ref)
    convolved(grad_ref[...], -1.0, back_ref)


def scan_kernel(states_ref, step_ref, out_ref):
    count = states_ref.shape[0]
    step = step_ref[...]
    zero = jnp.zeros(step.shape, jnp.float32)

    def up(j, carry):
        out_ref[j, 0, :, :] = carry.astype(jnp.bfloat16)
        return carry * step + states_ref[j, 0, :, :].astype(jnp.float32)

    lax.fori_loop(0, count, up, zero)

    def down(i, carry):
        j = count - 1 - i
        out_ref[j, 1, :, :] = carry.astype(jnp.bfloat16)
        return carry * step + states_ref[j, 1, :, :].astype(jnp.float32)

    lax.fori_loop(0, count, down, zero)


def apply_kernel(
    bound_ref, res_ref, rate_ref, fwd_ref, back_ref, key_ref, value_ref, cot_ref, in_ref, rim_ref,
    gm_ref, short_ref, ext, far,
):
    rows, width = cot_ref.shape
    modes = rate_ref.shape[0]
    taps = short_ref.shape[1]
    part = 32
    ids = row_ids()

    @pl.loop(0, width // LANES)
    def _(chunk):
        lanes = pl.ds(pl.multiple_of(chunk * LANES, LANES), LANES)
        fill_extended(ext, in_ref, rim_ref, lanes)
        before = bound_ref[0, :, lanes].astype(jnp.float32) * res_ref[:, lanes]
        after = bound_ref[1, :, lanes].astype(jnp.float32) * res_ref[:, lanes]
        ups = []
        downs = []
        steps = []
        for n in range(modes):
            rate = jnp.broadcast_to(rate_ref[n : n + 1, lanes], (8, LANES))
            ups.append(before[n : n + 1, :] * jnp.exp(-rate * (ids + 1.0)))
            downs.append(after[n : n + 1, :] * jnp.exp(-rate * (8.0 - ids)))
            steps.append(jnp.exp(-8.0 * rate))

        def summed(terms):
            total = list(terms)
            while len(total) > 1:
                total = [total[i] + total[i + 1] for i in range(0, len(total) - 1, 2)] + (
                    [total[-1]] if len(total) % 2 else []
                )
            return total[0]

        def body(block, carry):
            ups, downs = carry
            up = pl.ds(pl.multiple_of(block * 8, 8), 8)
            down = pl.ds(pl.multiple_of(rows - 8 - block * 8, 8), 8)
            far[0, up, :] = fwd_ref[up, lanes] + summed(ups)
            far[1, down, :] = back_ref[down, lanes] + summed(downs)
            return (
                tuple(t * s for t, s in zip(ups, steps)),
                tuple(t * s for t, s in zip(downs, steps)),
            )

        lax.fori_loop(0, rows // 8, body, (tuple(ups), tuple(downs)), unroll=2)

        sums = [[None] * taps for _ in range(3)]
        for first in range(0, rows, part):
            here = slice(first, first + part)
            mixer = far[0, here, :]
            back = far[1, here, :]
            grads = (
                cot_ref[here, lanes].astype(jnp.float32) * mixer,
                back * value_ref[here, lanes].astype(jnp.float32),
                back * key_ref[here, lanes].astype(jnp.float32),
            )
            for i in range(3):
                kept = grads[i].astype(jnp.bfloat16)
                gm_ref[i, here, lanes] = kept
                wide = kept.astype(jnp.float32)
                for j in range(taps):
                    term = wide * ext[i, first + RIM - j : first + RIM - j + part, :]
                    folded = jnp.sum(term.reshape(part // 8, 8, LANES), axis=0)
                    sums[i][j] = folded if sums[i][j] is None else sums[i][j] + folded
        for i in range(3):
            for j in range(taps):
                short_ref[i, j : j + 1, lanes] = jnp.sum(sums[i][j], axis=0, keepdims=True)


def spread_kernel(gm_ref, rim_ref, short_ref, out_ref, ext):
    rows, width = gm_ref.shape[1:]
    taps = short_ref.shape[1]
    part = 32

    @pl.loop(0, width // LANES)
    def _(chunk):
        lanes = pl.ds(pl.multiple_of(chunk * LANES, LANES), LANES)
        for i in range(3):
            ext[i, 0:rows, :] = gm_ref[i, :, lanes].astype(jnp.float32)
            ext[i, rows : rows + RIM, :] = rim_ref[i, :, lanes]
        for first in range(0, rows, part):
            for i in range(3):
                total = None
                for j in range(taps):
                    term = short_ref[i, j : j + 1, lanes] * ext[i, first + j : first + j + part, :]
                    total = term if total is None else total + term
                out_ref[i, first : first + part, lanes] = total.astype(jnp.bfloat16)


def tiled(shape, tile):
    lead = len(shape) - 1
    return pl.BlockSpec(tuple(shape[:-1]) + (tile,), lambda c: (0,) * lead + (c,))


def fixed(shape):
    return pl.BlockSpec(tuple(shape), lambda c: (0,) * len(shape))


def over_channels(kernel, operands, tables, outs, scratch, tile, flops):
    channels = operands[0].shape[-1]
    total_bytes = sum(a.size * a.dtype.itemsize for a in operands + tables)
    total_bytes += sum(math.prod(o.shape) * o.dtype.itemsize for o in outs)
    return pl.pallas_call(
        kernel,
        grid=(channels // tile,),
        in_specs=[tiled(a.shape, tile) for a in operands] + [fixed(a.shape) for a in tables],
        out_specs=[tiled(o.shape, tile) for o in outs],
        out_shape=outs,
        scratch_shapes=scratch,
        compiler_params=pltpu.CompilerParams(vmem_limit_bytes=VMEM_LIMIT),
        cost_estimate=pl.CostEstimate(flops=flops, bytes_accessed=total_bytes, transcendentals=0),
    )(*operands, *tables)


def per_device(inputs, cotangent, short_filter, residue, decay_rate):
    rows, channels = cotangent.shape
    modes = residue.shape[0]
    taps = short_filter.shape[1]
    ctx_count = lax.axis_size("ctx")
    narrow = channels // ctx_count
    tile = math.gcd(channels, 512)
    f32 = jnp.float32
    bf16 = jnp.bfloat16
    shape = jax.ShapeDtypeStruct
    high, low = split_table(spectral_table(rows))
    tables = [jnp.asarray(high), jnp.asarray(low)]
    turned = [jnp.asarray(np.ascontiguousarray(high.T)), jnp.asarray(np.ascontiguousarray(low.T))]
    ext_rows = pltpu.VMEM((3, rows + RIM, LANES), f32)

    rim = passed_along(inputs[:, rows - RIM :, :], "ctx", 1).astype(f32)
    (spec,) = over_channels(
        filter_kernel, [residue, decay_rate], tables,
        [shape((2 * rows, channels), f32)], [pltpu.VMEM((rows, tile), f32)], tile,
        6 * 2 * rows * rows * channels,
    )
    rim, spec = lax.optimization_barrier((rim, spec))
    gated, grad_mixer, key_mix, value_mix, states = over_channels(
        mix_kernel, [inputs, rim, cotangent, short_filter, decay_rate], [],
        [shape((rows, channels), bf16)] * 4 + [shape((2, modes, channels), bf16)],
        [ext_rows, pltpu.VMEM((2 * modes, LANES), f32)], tile, 110 * rows * channels,
    )
    sent = states.reshape(2, modes, ctx_count, narrow).transpose(2, 0, 1, 3)
    arrived = lax.all_to_all(sent, "ctx", split_axis=0, concat_axis=0, tiled=True)
    fwd_part, back_part = over_channels(
        local_kernel, [gated, grad_mixer, spec], tables + turned,
        [shape((rows, channels), f32)] * 2, [], tile, 16 * 2 * rows * rows * channels,
    )
    first_chan = lax.axis_index("ctx") * narrow
    rate_part = lax.dynamic_slice_in_dim(decay_rate, first_chan, narrow, 1)
    bounds = pl.pallas_call(
        scan_kernel,
        out_shape=shape(arrived.shape, bf16),
        compiler_params=pltpu.CompilerParams(vmem_limit_bytes=VMEM_LIMIT),
    )(arrived, jnp.exp(-rate_part * rows))
    returned = lax.all_to_all(bounds, "ctx", split_axis=0, concat_axis=0, tiled=True)
    bound = returned.transpose(1, 2, 0, 3).reshape(2, modes, channels)
    grad_mix, short_grad = over_channels(
        apply_kernel,
        [bound, residue, decay_rate, fwd_part, back_part, key_mix, value_mix, cotangent, inputs, rim],
        [],
        [shape((3, rows, channels), bf16), shape((3, taps, channels), f32)],
        [ext_rows, pltpu.VMEM((2, rows, LANES), f32)], tile, 110 * rows * channels,
    )
    next_rim = passed_along(grad_mix[:, :RIM, :], "ctx", -1)
    terms = short_grad.reshape(3 * taps, ctx_count, narrow).transpose(1, 0, 2)
    terms = lax.all_to_all(terms, "ctx", split_axis=0, concat_axis=0, tiled=True)
    next_rim, terms = lax.optimization_barrier((next_rim, terms))
    next_rim = next_rim.astype(f32)
    own_sum = jnp.sum(terms, axis=0)
    own_squares = jnp.broadcast_to(jnp.sum(own_sum * own_sum), (1, narrow))
    packed = jnp.concatenate([own_sum, own_squares], axis=0)
    packed = jnp.broadcast_to(packed[None], (ctx_count,) + packed.shape)
    packed = lax.all_to_all(packed, "ctx", split_axis=0, concat_axis=0, tiled=True)
    short_sum = packed[:, : 3 * taps].transpose(1, 0, 2).reshape(3, taps, channels)
    (grad_inputs,) = over_channels(
        spread_kernel, [grad_mix, next_rim, short_filter], [],
        [shape((3, rows, channels), bf16)], [ext_rows], tile, 42 * rows * channels,
    )
    squares = lax.psum(jnp.sum(packed[:, 3 * taps, 0]), "tp")
    clip_limit = math.sqrt(3 * channels * lax.axis_size("tp") * taps)
    factor = jnp.minimum(1.0, clip_limit / (jnp.sqrt(squares) + 1e-06))
    return (grad_inputs, short_sum * factor)


def solution(mesh):
    return jax.shard_map(
        per_device,
        mesh=mesh,
        in_specs=(
            P(None, "ctx", "tp"),
            P("ctx", "tp"),
            P(None, None, "tp"),
            P(None, "tp"),
            P(None, "tp"),
        ),
        out_specs=(P(None, "ctx", "tp"), P(None, None, "tp")),
        check_vma=False,
    )
```

```python
import functools
import math

import jax
import jax.numpy as jnp
import numpy as np
from jax import lax
from jax.experimental import pallas as pl
from jax.experimental.pallas import tpu as pltpu
from jax.sharding import PartitionSpec as P

LANES = 128
RIM = 8
VMEM_LIMIT = 60 * 1024 * 1024


def passed_along(shard, axis, by):
    length = lax.axis_size(axis)
    pairs = [(i, i + by) for i in range(length) if 0 <= i + by < length]
    return lax.ppermute(shard, axis, pairs)


def spectral_table(rows):
    frame = 2 * rows
    freq = np.arange(rows)[:, None]
    pos = np.arange(rows)[None, :]
    angles = (freq * pos % frame) * (2.0 * math.pi / frame)
    lower = -np.sin(angles)
    lower[0] = 1.0 - 2.0 * (np.arange(rows) % 2)
    return np.concatenate([np.cos(angles), lower], axis=0).astype(np.float32)


def split_table(table):
    high = table.astype(jnp.bfloat16)
    low = (table - high.astype(np.float32)).astype(jnp.bfloat16)
    return high, low


def mm(a, b):
    return jnp.dot(a, b, preferred_element_type=jnp.float32)


def row_ids():
    return lax.broadcasted_iota(jnp.int32, (8, LANES), 0).astype(jnp.float32)


def filter_kernel(res_ref, rate_ref, high_ref, low_ref, spec_ref, taps):
    modes, width = res_ref.shape
    rows = taps.shape[0]
    ids = row_ids()

    @pl.loop(0, width // LANES)
    def _(chunk):
        lanes = pl.ds(pl.multiple_of(chunk * LANES, LANES), LANES)
        terms = []
        steps = []
        for n in range(modes):
            rate = jnp.broadcast_to(rate_ref[n : n + 1, lanes], (8, LANES))
            terms.append(res_ref[n : n + 1, lanes] * jnp.exp(-rate * ids))
            steps.append(jnp.exp(-8.0 * rate))

        def body(block, terms):
            total = list(terms)
            while len(total) > 1:
                total = [total[i] + total[i + 1] for i in range(0, len(total) - 1, 2)] + (
                    [total[-1]] if len(total) % 2 else []
                )
            taps[pl.ds(pl.multiple_of(block * 8, 8), 8), lanes] = total[0]
            return tuple(t * s for t, s in zip(terms, steps))

        lax.fori_loop(0, rows // 8, body, tuple(terms), unroll=4)

    whole = taps[...]
    main = whole.astype(jnp.bfloat16)
    rest = (whole - main.astype(jnp.float32)).astype(jnp.bfloat16)
    spec = mm(high_ref[...], main) + (mm(low_ref[...], main) + mm(high_ref[...], rest))
    index = lax.broadcasted_iota(jnp.int32, spec.shape, 0)
    edge = jnp.logical_or(index == 0, index == rows)
    spec_ref[...] = spec * jnp.where(edge, 0.5 / rows, 1.0 / rows)


def fill_extended(ext, in_ref, rim_ref, lanes):
    rows = in_ref.shape[1]
    for i in range(3):
        ext[i, 0:RIM, :] = rim_ref[i, :, lanes]
        ext[i, RIM : RIM + rows, :] = in_ref[i, :, lanes].astype(jnp.float32)


def mix_kernel(
    in_ref, rim_ref, cot_ref, short_ref, rate_ref,
    gated_ref, grad_ref, key_ref, value_ref, state_ref, rowed,
):
    rows, width = cot_ref.shape
    modes = rate_ref.shape[0]
    taps = short_ref.shape[1]
    part = 32
    ids = row_ids()

    @pl.loop(0, width // LANES)
    def _(chunk):
        lanes = pl.ds(pl.multiple_of(chunk * LANES, LANES), LANES)
        for first in range(0, rows, part):
            mixed = []
            for i in range(3):
                own = in_ref[i, first : first + part, lanes].astype(jnp.float32)
                if first > 0:
                    prior = in_ref[i, first - 16 : first, lanes].astype(jnp.float32)[16 - RIM : 16]
                else:
                    prior = rim_ref[i, :, lanes]
                both = jnp.concatenate([prior, own], axis=0)
                total = short_ref[i, 0:1, lanes] * own
                for j in range(1, taps):
                    moved = pltpu.roll(both, j, 0)[RIM : RIM + part]
                    total = total + short_ref[i, j : j + 1, lanes] * moved
                mixed.append(total)
            here = slice(first, first + part)
            gated_ref[here, lanes] = (mixed[1] * mixed[2]).astype(jnp.bfloat16)
            grad_ref[here, lanes] = (cot_ref[here, lanes].astype(jnp.float32) * mixed[0]).astype(jnp.bfloat16)
            key_ref[here, lanes] = mixed[1].astype(jnp.bfloat16)
            value_ref[here, lanes] = mixed[2].astype(jnp.bfloat16)

        steps = [
            jnp.exp(-8.0 * jnp.broadcast_to(rate_ref[n : n + 1, lanes], (8, LANES)))
            for n in range(modes)
        ]

        def body(block, carry):
            ends, starts = carry
            up = pl.multiple_of(block * 16, 16)
            down = pl.multiple_of(rows - 16 - block * 16, 16)
            ahead = gated_ref[pl.ds(up, 16), lanes].astype(jnp.float32)
            behind = grad_ref[pl.ds(down, 16), lanes].astype(jnp.float32)
            ends = [e * s + ahead[0:8] for e, s in zip(ends, steps)]
            starts = [e * s + behind[8:16] for e, s in zip(starts, steps)]
            ends = [e * s + ahead[8:16] for e, s in zip(ends, steps)]
            starts = [e * s + behind[0:8] for e, s in zip(starts, steps)]
            return tuple(ends), tuple(starts)

        zero = tuple(jnp.zeros((8, LANES), jnp.float32) for _ in range(modes))
        ends, starts = lax.fori_loop(0, rows // 16, body, (zero, zero), unroll=2)
        for n in range(modes):
            rate = jnp.broadcast_to(rate_ref[n : n + 1, lanes], (8, LANES))
            rowed[n : n + 1, :] = jnp.sum(ends[n] * jnp.exp(-rate * (7.0 - ids)), axis=0, keepdims=True)
            rowed[modes + n : modes + n + 1, :] = jnp.sum(
                starts[n] * jnp.exp(-rate * ids), axis=0, keepdims=True
            )
        state_ref[0, :, lanes] = rowed[0:modes, :].astype(jnp.bfloat16)
        state_ref[1, :, lanes] = rowed[modes : 2 * modes, :].astype(jnp.bfloat16)


def local_kernel(sign, signal_ref, spec_ref, high_ref, low_ref, hight_ref, lowt_ref, out_ref):
    rows = signal_ref.shape[0]
    real = spec_ref[0:rows, :]
    lower = spec_ref[rows : 2 * rows, :]
    first = lax.broadcasted_iota(jnp.int32, real.shape, 0) == 0
    imag = sign * jnp.where(first, 0.0, lower)
    other = jnp.where(first, lower, real)
    seen = mm(high_ref[...], signal_ref[...]) + mm(low_ref[...], signal_ref[...])
    a = seen[0:rows, :]
    b = seen[rows : 2 * rows, :]
    top = (a * real - b * imag).astype(jnp.bfloat16)
    bottom = (a * imag + b * other).astype(jnp.bfloat16)
    both = jnp.concatenate([top, bottom], axis=0)
    out_ref[...] = mm(hight_ref[...], both) + mm(lowt_ref[...], both)


def scan_kernel(states_ref, step_ref, out_ref):
    count = states_ref.shape[0]
    step = step_ref[...]
    zero = jnp.zeros(step.shape, jnp.float32)

    def up(j, carry):
        out_ref[j, 0, :, :] = carry.astype(jnp.bfloat16)
        return carry * step + states_ref[j, 0, :, :].astype(jnp.float32)

    lax.fori_loop(0, count, up, zero)

    def down(i, carry):
        j = count - 1 - i
        out_ref[j, 1, :, :] = carry.astype(jnp.bfloat16)
        return carry * step + states_ref[j, 1, :, :].astype(jnp.float32)

    lax.fori_loop(0, count, down, zero)


def apply_kernel(
    bound_ref, res_ref, rate_ref, fwd_ref, back_ref, key_ref, value_ref, cot_ref, in_ref, rim_ref,
    gm_ref, short_ref, ext, far,
):
    rows, width = cot_ref.shape
    modes = rate_ref.shape[0]
    taps = short_ref.shape[1]
    part = 32
    ids = row_ids()

    @pl.loop(0, width // LANES)
    def _(chunk):
        lanes = pl.ds(pl.multiple_of(chunk * LANES, LANES), LANES)
        fill_extended(ext, in_ref, rim_ref, lanes)
        before = bound_ref[0, :, lanes].astype(jnp.float32) * res_ref[:, lanes]
        after = bound_ref[1, :, lanes].astype(jnp.float32) * res_ref[:, lanes]
        ups = []
        downs = []
        steps = []
        for n in range(modes):
            rate = jnp.broadcast_to(rate_ref[n : n + 1, lanes], (8, LANES))
            ups.append(before[n : n + 1, :] * jnp.exp(-rate * (ids + 1.0)))
            downs.append(after[n : n + 1, :] * jnp.exp(-rate * (8.0 - ids)))
            steps.append(jnp.exp(-8.0 * rate))

        def summed(terms):
            total = list(terms)
            while len(total) > 1:
                total = [total[i] + total[i + 1] for i in range(0, len(total) - 1, 2)] + (
                    [total[-1]] if len(total) % 2 else []
                )
            return total[0]

        def body(block, carry):
            ups, downs = carry
            up = pl.ds(pl.multiple_of(block * 8, 8), 8)
            down = pl.ds(pl.multiple_of(rows - 8 - block * 8, 8), 8)
            far[0, up, :] = fwd_ref[up, lanes] + summed(ups)
            far[1, down, :] = back_ref[down, lanes] + summed(downs)
            return (
                tuple(t * s for t, s in zip(ups, steps)),
                tuple(t * s for t, s in zip(downs, steps)),
            )

        lax.fori_loop(0, rows // 8, body, (tuple(ups), tuple(downs)), unroll=2)

        sums = [[None] * taps for _ in range(3)]
        for first in range(0, rows, part):
            here = slice(first, first + part)
            mixer = far[0, here, :]
            back = far[1, here, :]
            grads = (
                cot_ref[here, lanes].astype(jnp.float32) * mixer,
                back * value_ref[here, lanes].astype(jnp.float32),
                back * key_ref[here, lanes].astype(jnp.float32),
            )
            for i in range(3):
                kept = grads[i].astype(jnp.bfloat16)
                gm_ref[i, here, lanes] = kept
                wide = kept.astype(jnp.float32)
                for j in range(taps):
                    term = wide * ext[i, first + RIM - j : first + RIM - j + part, :]
                    folded = jnp.sum(term.reshape(part // 8, 8, LANES), axis=0)
                    sums[i][j] = folded if sums[i][j] is None else sums[i][j] + folded
        for i in range(3):
            for j in range(taps):
                short_ref[i, j : j + 1, lanes] = jnp.sum(sums[i][j], axis=0, keepdims=True)


def spread_kernel(gm_ref, rim_ref, short_ref, out_ref):
    rows, width = gm_ref.shape[1:]
    taps = short_ref.shape[1]
    part = 64

    @pl.loop(0, width // LANES)
    def _(chunk):
        lanes = pl.ds(pl.multiple_of(chunk * LANES, LANES), LANES)
        for first in range(0, rows, part):
            end = first + part
            for i in range(3):
                own = gm_ref[i, first:end, lanes].astype(jnp.float32)
                if end < rows:
                    beyond = gm_ref[i, end : end + 16, lanes].astype(jnp.float32)[0:RIM]
                else:
                    beyond = rim_ref[i, :, lanes]
                both = jnp.concatenate([own, beyond], axis=0)
                total = short_ref[i, 0:1, lanes] * own
                for j in range(1, taps):
                    moved = pltpu.roll(both, part + RIM - j, 0)[0:part]
                    total = total + short_ref[i, j : j + 1, lanes] * moved
                out_ref[i, first:end, lanes] = total.astype(jnp.bfloat16)


def tiled(shape, tile):
    lead = len(shape) - 1
    return pl.BlockSpec(tuple(shape[:-1]) + (tile,), lambda c: (0,) * lead + (c,))


def fixed(shape):
    return pl.BlockSpec(tuple(shape), lambda c: (0,) * len(shape))


def over_channels(kernel, operands, tables, outs, scratch, tile, flops):
    channels = operands[0].shape[-1]
    total_bytes = sum(a.size * a.dtype.itemsize for a in operands + tables)
    total_bytes += sum(math.prod(o.shape) * o.dtype.itemsize for o in outs)
    return pl.pallas_call(
        kernel,
        grid=(channels // tile,),
        in_specs=[tiled(a.shape, tile) for a in operands] + [fixed(a.shape) for a in tables],
        out_specs=[tiled(o.shape, tile) for o in outs],
        out_shape=outs,
        scratch_shapes=scratch,
        compiler_params=pltpu.CompilerParams(vmem_limit_bytes=VMEM_LIMIT),
        cost_estimate=pl.CostEstimate(flops=flops, bytes_accessed=total_bytes, transcendentals=0),
    )(*operands, *tables)


def per_device(inputs, cotangent, short_filter, residue, decay_rate):
    rows, channels = cotangent.shape
    modes = residue.shape[0]
    taps = short_filter.shape[1]
    ctx_count = lax.axis_size("ctx")
    narrow = channels // ctx_count
    tile = math.gcd(channels, 512)
    f32 = jnp.float32
    bf16 = jnp.bfloat16
    shape = jax.ShapeDtypeStruct
    high, low = split_table(spectral_table(rows))
    tables = [jnp.asarray(high), jnp.asarray(low)]
    turned = [jnp.asarray(np.ascontiguousarray(high.T)), jnp.asarray(np.ascontiguousarray(low.T))]
    ext_rows = pltpu.VMEM((3, rows + RIM, LANES), f32)

    rim = passed_along(inputs[:, rows - RIM :, :], "ctx", 1).astype(f32)
    (spec,) = over_channels(
        filter_kernel, [residue, decay_rate], tables,
        [shape((2 * rows, channels), f32)], [pltpu.VMEM((rows, tile), f32)], tile,
        6 * 2 * rows * rows * channels,
    )
    rim, spec = lax.optimization_barrier((rim, spec))
    gated, grad_mixer, key_mix, value_mix, states = over_channels(
        mix_kernel, [inputs, rim, cotangent, short_filter, decay_rate], [],
        [shape((rows, channels), bf16)] * 4 + [shape((2, modes, channels), bf16)],
        [pltpu.VMEM((2 * modes, LANES), f32)], tile, 110 * rows * channels,
    )
    sent = states.reshape(2, modes, ctx_count, narrow).transpose(2, 0, 1, 3)
    arrived = lax.all_to_all(sent, "ctx", split_axis=0, concat_axis=0, tiled=True)
    def local(sign, signal):
        return over_channels(
            functools.partial(local_kernel, sign), [signal, spec], tables + turned,
            [shape((rows, channels), f32)], [], tile, 8 * 2 * rows * rows * channels,
        )[0]

    fwd_part = local(1.0, gated)
    arrived, fwd_part = lax.optimization_barrier((arrived, fwd_part))
    first_chan = lax.axis_index("ctx") * narrow
    rate_part = lax.dynamic_slice_in_dim(decay_rate, first_chan, narrow, 1)
    bounds = pl.pallas_call(
        scan_kernel,
        out_shape=shape(arrived.shape, bf16),
        compiler_params=pltpu.CompilerParams(vmem_limit_bytes=VMEM_LIMIT),
    )(arrived, jnp.exp(-rate_part * rows))
    returned = lax.all_to_all(bounds, "ctx", split_axis=0, concat_axis=0, tiled=True)
    back_part = local(-1.0, grad_mixer)
    returned, back_part = lax.optimization_barrier((returned, back_part))
    bound = returned.transpose(1, 2, 0, 3).reshape(2, modes, channels)
    grad_mix, short_grad = over_channels(
        apply_kernel,
        [bound, residue, decay_rate, fwd_part, back_part, key_mix, value_mix, cotangent, inputs, rim],
        [],
        [shape((3, rows, channels), bf16), shape((3, taps, channels), f32)],
        [ext_rows, pltpu.VMEM((2, rows, LANES), f32)], tile, 110 * rows * channels,
    )
    next_rim = passed_along(grad_mix[:, :RIM, :], "ctx", -1)
    terms = short_grad.reshape(3 * taps, ctx_count, narrow).transpose(1, 0, 2)
    terms = lax.all_to_all(terms, "ctx", split_axis=0, concat_axis=0, tiled=True)
    next_rim, terms = lax.optimization_barrier((next_rim, terms))
    next_rim = next_rim.astype(f32)
    own_sum = jnp.sum(terms, axis=0)
    own_squares = jnp.broadcast_to(jnp.sum(own_sum * own_sum), (1, narrow))
    packed = jnp.concatenate([own_sum, own_squares], axis=0)
    packed = jnp.broadcast_to(packed[None], (ctx_count,) + packed.shape)
    packed = lax.all_to_all(packed, "ctx", split_axis=0, concat_axis=0, tiled=True)
    (grad_inputs,) = over_channels(
        spread_kernel, [grad_mix, next_rim, short_filter], [],
        [shape((3, rows, channels), bf16)], [], tile, 42 * rows * channels,
    )
    packed, grad_inputs = lax.optimization_barrier((packed, grad_inputs))
    short_sum = packed[:, : 3 * taps].transpose(1, 0, 2).reshape(3, taps, channels)
    squares = lax.psum(jnp.sum(packed[:, 3 * taps, 0]), "tp")
    clip_limit = math.sqrt(3 * channels * lax.axis_size("tp") * taps)
    factor = jnp.minimum(1.0, clip_limit / (jnp.sqrt(squares) + 1e-06))
    return (grad_inputs, short_sum * factor)


def solution(mesh):
    return jax.shard_map(
        per_device,
        mesh=mesh,
        in_specs=(
            P(None, "ctx", "tp"),
            P("ctx", "tp"),
            P(None, None, "tp"),
            P(None, "tp"),
            P(None, "tp"),
        ),
        out_specs=(P(None, "ctx", "tp"), P(None, None, "tp")),
        check_vma=False,
    )
```

```python
import functools
import math

import jax
import jax.numpy as jnp
import numpy as np
from jax import lax
from jax.experimental import pallas as pl
from jax.experimental.pallas import tpu as pltpu
from jax.sharding import PartitionSpec as P

LANES = 128
RIM = 8
VMEM_LIMIT = 60 * 1024 * 1024


def passed_along(shard, axis, by):
    length = lax.axis_size(axis)
    pairs = [(i, i + by) for i in range(length) if 0 <= i + by < length]
    return lax.ppermute(shard, axis, pairs)


def spectral_table(rows):
    frame = 2 * rows
    freq = np.arange(rows)[:, None]
    pos = np.arange(rows)[None, :]
    angles = (freq * pos % frame) * (2.0 * math.pi / frame)
    lower = -np.sin(angles)
    lower[0] = 1.0 - 2.0 * (np.arange(rows) % 2)
    return np.concatenate([np.cos(angles), lower], axis=0).astype(np.float32)


def split_table(table):
    high = table.astype(jnp.bfloat16)
    low = (table - high.astype(np.float32)).astype(jnp.bfloat16)
    return high, low


def mm(a, b):
    return jnp.dot(a, b, preferred_element_type=jnp.float32)


def row_ids():
    return lax.broadcasted_iota(jnp.int32, (8, LANES), 0).astype(jnp.float32)


def filter_kernel(res_ref, rate_ref, high_ref, low_ref, spec_ref, taps):
    modes, width = res_ref.shape
    rows = taps.shape[0]
    ids = row_ids()

    @pl.loop(0, width // LANES)
    def _(chunk):
        lanes = pl.ds(pl.multiple_of(chunk * LANES, LANES), LANES)
        terms = []
        steps = []
        for n in range(modes):
            rate = jnp.broadcast_to(rate_ref[n : n + 1, lanes], (8, LANES))
            terms.append(res_ref[n : n + 1, lanes] * jnp.exp(-rate * ids))
            steps.append(jnp.exp(-8.0 * rate))

        def body(block, terms):
            total = list(terms)
            while len(total) > 1:
                total = [total[i] + total[i + 1] for i in range(0, len(total) - 1, 2)] + (
                    [total[-1]] if len(total) % 2 else []
                )
            taps[pl.ds(pl.multiple_of(block * 8, 8), 8), lanes] = total[0]
            return tuple(t * s for t, s in zip(terms, steps))

        lax.fori_loop(0, rows // 8, body, tuple(terms), unroll=4)

    whole = taps[...]
    main = whole.astype(jnp.bfloat16)
    rest = (whole - main.astype(jnp.float32)).astype(jnp.bfloat16)
    spec = mm(high_ref[...], main) + (mm(low_ref[...], main) + mm(high_ref[...], rest))
    index = lax.broadcasted_iota(jnp.int32, spec.shape, 0)
    edge = jnp.logical_or(index == 0, index == rows)
    spec_ref[...] = spec * jnp.where(edge, 0.5 / rows, 1.0 / rows)


def fill_extended(ext, in_ref, rim_ref, lanes):
    rows = in_ref.shape[1]
    for i in range(3):
        ext[i, 0:RIM, :] = rim_ref[i, :, lanes]
        ext[i, RIM : RIM + rows, :] = in_ref[i, :, lanes].astype(jnp.float32)


def mix_kernel(
    in_ref, rim_ref, cot_ref, short_ref, rate_ref,
    gated_ref, grad_ref, key_ref, value_ref, state_ref, ext, rowed,
):
    rows, width = cot_ref.shape
    modes = rate_ref.shape[0]
    taps = short_ref.shape[1]
    half = (taps + 1) // 2
    part = 64
    ids = row_ids()

    @pl.loop(0, width // LANES)
    def _(chunk):
        lanes = pl.ds(pl.multiple_of(chunk * LANES, LANES), LANES)
        for i in range(3):
            ext[i, 0:RIM, :] = jnp.zeros((RIM, LANES), jnp.float32)
            ext[i, RIM : 2 * RIM, :] = rim_ref[i, :, lanes]
            ext[i, 2 * RIM : 2 * RIM + rows, :] = in_ref[i, :, lanes].astype(jnp.float32)
        for first in range(0, rows, part):
            mixed = []
            for i in range(3):
                near = None
                far = None
                for m in range(half):
                    seen = ext[i, first + RIM - m : first + 2 * RIM - m + part, :]
                    term = short_ref[i, m : m + 1, lanes] * seen[RIM:]
                    near = term if near is None else near + term
                    if half + m < taps:
                        term = short_ref[i, half + m : half + m + 1, lanes] * seen
                        far = term if far is None else far + term
                mixed.append(near + pltpu.roll(far, half, 0)[RIM:])
            here = slice(first, first + part)
            gated_ref[here, lanes] = (mixed[1] * mixed[2]).astype(jnp.bfloat16)
            grad_ref[here, lanes] = (cot_ref[here, lanes].astype(jnp.float32) * mixed[0]).astype(jnp.bfloat16)
            key_ref[here, lanes] = mixed[1].astype(jnp.bfloat16)
            value_ref[here, lanes] = mixed[2].astype(jnp.bfloat16)

        steps = [
            jnp.exp(-8.0 * jnp.broadcast_to(rate_ref[n : n + 1, lanes], (8, LANES)))
            for n in range(modes)
        ]

        def body(block, carry):
            ends, starts = carry
            up = pl.multiple_of(block * 16, 16)
            down = pl.multiple_of(rows - 16 - block * 16, 16)
            ahead = gated_ref[pl.ds(up, 16), lanes].astype(jnp.float32)
            behind = grad_ref[pl.ds(down, 16), lanes].astype(jnp.float32)
            ends = [e * s + ahead[0:8] for e, s in zip(ends, steps)]
            starts = [e * s + behind[8:16] for e, s in zip(starts, steps)]
            ends = [e * s + ahead[8:16] for e, s in zip(ends, steps)]
            starts = [e * s + behind[0:8] for e, s in zip(starts, steps)]
            return tuple(ends), tuple(starts)

        zero = tuple(jnp.zeros((8, LANES), jnp.float32) for _ in range(modes))
        ends, starts = lax.fori_loop(0, rows // 16, body, (zero, zero), unroll=2)
        for n in range(modes):
            rate = jnp.broadcast_to(rate_ref[n : n + 1, lanes], (8, LANES))
            rowed[n : n + 1, :] = jnp.sum(ends[n] * jnp.exp(-rate * (7.0 - ids)), axis=0, keepdims=True)
            rowed[modes + n : modes + n + 1, :] = jnp.sum(
                starts[n] * jnp.exp(-rate * ids), axis=0, keepdims=True
            )
        state_ref[0, :, lanes] = rowed[0:modes, :].astype(jnp.bfloat16)
        state_ref[1, :, lanes] = rowed[modes : 2 * modes, :].astype(jnp.bfloat16)


def local_kernel(sign, signal_ref, spec_ref, high_ref, low_ref, hight_ref, lowt_ref, out_ref):
    rows = signal_ref.shape[0]
    real = spec_ref[0:rows, :]
    lower = spec_ref[rows : 2 * rows, :]
    first = lax.broadcasted_iota(jnp.int32, real.shape, 0) == 0
    imag = sign * jnp.where(first, 0.0, lower)
    other = jnp.where(first, lower, real)
    seen = mm(high_ref[...], signal_ref[...]) + mm(low_ref[...], signal_ref[...])
    a = seen[0:rows, :]
    b = seen[rows : 2 * rows, :]
    top = (a * real - b * imag).astype(jnp.bfloat16)
    bottom = (a * imag + b * other).astype(jnp.bfloat16)
    both = jnp.concatenate([top, bottom], axis=0)
    out_ref[...] = mm(hight_ref[...], both) + mm(lowt_ref[...], both)


def scan_kernel(states_ref, step_ref, out_ref):
    count = states_ref.shape[0]
    step = step_ref[...]
    zero = jnp.zeros(step.shape, jnp.float32)

    def up(j, carry):
        out_ref[j, 0, :, :] = carry.astype(jnp.bfloat16)
        return carry * step + states_ref[j, 0, :, :].astype(jnp.float32)

    lax.fori_loop(0, count, up, zero)

    def down(i, carry):
        j = count - 1 - i
        out_ref[j, 1, :, :] = carry.astype(jnp.bfloat16)
        return carry * step + states_ref[j, 1, :, :].astype(jnp.float32)

    lax.fori_loop(0, count, down, zero)


def apply_kernel(
    bound_ref, res_ref, rate_ref, fwd_ref, back_ref, key_ref, value_ref, cot_ref, in_ref, rim_ref,
    gm_ref, short_ref, ext, far,
):
    rows, width = cot_ref.shape
    modes = rate_ref.shape[0]
    taps = short_ref.shape[1]
    part = 32
    ids = row_ids()

    @pl.loop(0, width // LANES)
    def _(chunk):
        lanes = pl.ds(pl.multiple_of(chunk * LANES, LANES), LANES)
        fill_extended(ext, in_ref, rim_ref, lanes)
        before = bound_ref[0, :, lanes].astype(jnp.float32) * res_ref[:, lanes]
        after = bound_ref[1, :, lanes].astype(jnp.float32) * res_ref[:, lanes]
        ups = []
        downs = []
        steps = []
        for n in range(modes):
            rate = jnp.broadcast_to(rate_ref[n : n + 1, lanes], (8, LANES))
            ups.append(before[n : n + 1, :] * jnp.exp(-rate * (ids + 1.0)))
            downs.append(after[n : n + 1, :] * jnp.exp(-rate * (8.0 - ids)))
            steps.append(jnp.exp(-8.0 * rate))

        def summed(terms):
            total = list(terms)
            while len(total) > 1:
                total = [total[i] + total[i + 1] for i in range(0, len(total) - 1, 2)] + (
                    [total[-1]] if len(total) % 2 else []
                )
            return total[0]

        def body(block, carry):
            ups, downs = carry
            up = pl.ds(pl.multiple_of(block * 8, 8), 8)
            down = pl.ds(pl.multiple_of(rows - 8 - block * 8, 8), 8)
            far[0, up, :] = fwd_ref[up, lanes] + summed(ups)
            far[1, down, :] = back_ref[down, lanes] + summed(downs)
            return (
                tuple(t * s for t, s in zip(ups, steps)),
                tuple(t * s for t, s in zip(downs, steps)),
            )

        lax.fori_loop(0, rows // 8, body, (tuple(ups), tuple(downs)), unroll=2)

        sums = [[None] * taps for _ in range(3)]
        for first in range(0, rows, part):
            here = slice(first, first + part)
            mixer = far[0, here, :]
            back = far[1, here, :]
            grads = (
                cot_ref[here, lanes].astype(jnp.float32) * mixer,
                back * value_ref[here, lanes].astype(jnp.float32),
                back * key_ref[here, lanes].astype(jnp.float32),
            )
            for i in range(3):
                kept = grads[i].astype(jnp.bfloat16)
                gm_ref[i, here, lanes] = kept
                wide = kept.astype(jnp.float32)
                for j in range(taps):
                    term = wide * ext[i, first + RIM - j : first + RIM - j + part, :]
                    folded = jnp.sum(term.reshape(part // 8, 8, LANES), axis=0)
                    sums[i][j] = folded if sums[i][j] is None else sums[i][j] + folded
        for i in range(3):
            for j in range(taps):
                short_ref[i, j : j + 1, lanes] = jnp.sum(sums[i][j], axis=0, keepdims=True)


def spread_kernel(gm_ref, rim_ref, short_ref, out_ref, ext):
    rows, width = gm_ref.shape[1:]
    taps = short_ref.shape[1]
    half = (taps + 1) // 2
    part = 64

    @pl.loop(0, width // LANES)
    def _(chunk):
        lanes = pl.ds(pl.multiple_of(chunk * LANES, LANES), LANES)
        for i in range(3):
            ext[i, 0:rows, :] = gm_ref[i, :, lanes].astype(jnp.float32)
            ext[i, rows : rows + RIM, :] = rim_ref[i, :, lanes]
            ext[i, rows + RIM : rows + 2 * RIM, :] = jnp.zeros((RIM, LANES), jnp.float32)
        for first in range(0, rows, part):
            for i in range(3):
                near = None
                far = None
                for m in range(half):
                    seen = ext[i, first + m : first + m + part + RIM, :]
                    term = short_ref[i, m : m + 1, lanes] * seen[0:part]
                    near = term if near is None else near + term
                    if half + m < taps:
                        term = short_ref[i, half + m : half + m + 1, lanes] * seen
                        far = term if far is None else far + term
                total = near + pltpu.roll(far, part + RIM - half, 0)[0:part]
                out_ref[i, first : first + part, lanes] = total.astype(jnp.bfloat16)


def tiled(shape, tile):
    lead = len(shape) - 1
    return pl.BlockSpec(tuple(shape[:-1]) + (tile,), lambda c: (0,) * lead + (c,))


def fixed(shape):
    return pl.BlockSpec(tuple(shape), lambda c: (0,) * len(shape))


def over_channels(kernel, operands, tables, outs, scratch, tile, flops):
    channels = operands[0].shape[-1]
    total_bytes = sum(a.size * a.dtype.itemsize for a in operands + tables)
    total_bytes += sum(math.prod(o.shape) * o.dtype.itemsize for o in outs)
    return pl.pallas_call(
        kernel,
        grid=(channels // tile,),
        in_specs=[tiled(a.shape, tile) for a in operands] + [fixed(a.shape) for a in tables],
        out_specs=[tiled(o.shape, tile) for o in outs],
        out_shape=outs,
        scratch_shapes=scratch,
        compiler_params=pltpu.CompilerParams(vmem_limit_bytes=VMEM_LIMIT),
        cost_estimate=pl.CostEstimate(flops=flops, bytes_accessed=total_bytes, transcendentals=0),
    )(*operands, *tables)


def per_device(inputs, cotangent, short_filter, residue, decay_rate):
    rows, channels = cotangent.shape
    modes = residue.shape[0]
    taps = short_filter.shape[1]
    ctx_count = lax.axis_size("ctx")
    narrow = channels // ctx_count
    tile = math.gcd(channels, 512)
    f32 = jnp.float32
    bf16 = jnp.bfloat16
    shape = jax.ShapeDtypeStruct
    high, low = split_table(spectral_table(rows))
    tables = [jnp.asarray(high), jnp.asarray(low)]
    turned = [jnp.asarray(np.ascontiguousarray(high.T)), jnp.asarray(np.ascontiguousarray(low.T))]
    padded_rows = pltpu.VMEM((3, rows + 2 * RIM, LANES), f32)
    ext_rows = pltpu.VMEM((3, rows + RIM, LANES), f32)

    rim = passed_along(inputs[:, rows - RIM :, :], "ctx", 1).astype(f32)
    (spec,) = over_channels(
        filter_kernel, [residue, decay_rate], tables,
        [shape((2 * rows, channels), f32)], [pltpu.VMEM((rows, tile), f32)], tile,
        6 * 2 * rows * rows * channels,
    )
    rim, spec = lax.optimization_barrier((rim, spec))
    gated, grad_mixer, key_mix, value_mix, states = over_channels(
        mix_kernel, [inputs, rim, cotangent, short_filter, decay_rate], [],
        [shape((rows, channels), bf16)] * 4 + [shape((2, modes, channels), bf16)],
        [padded_rows, pltpu.VMEM((2 * modes, LANES), f32)], tile, 110 * rows * channels,
    )
    sent = states.reshape(2, modes, ctx_count, narrow).transpose(2, 0, 1, 3)
    arrived = lax.all_to_all(sent, "ctx", split_axis=0, concat_axis=0, tiled=True)
    def local(sign, signal):
        return over_channels(
            functools.partial(local_kernel, sign), [signal, spec], tables + turned,
            [shape((rows, channels), f32)], [], tile, 8 * 2 * rows * rows * channels,
        )[0]

    fwd_part = local(1.0, gated)
    arrived, fwd_part = lax.optimization_barrier((arrived, fwd_part))
    first_chan = lax.axis_index("ctx") * narrow
    rate_part = lax.dynamic_slice_in_dim(decay_rate, first_chan, narrow, 1)
    bounds = pl.pallas_call(
        scan_kernel,
        out_shape=shape(arrived.shape, bf16),
        compiler_params=pltpu.CompilerParams(vmem_limit_bytes=VMEM_LIMIT),
    )(arrived, jnp.exp(-rate_part * rows))
    returned = lax.all_to_all(bounds, "ctx", split_axis=0, concat_axis=0, tiled=True)
    back_part = local(-1.0, grad_mixer)
    returned, back_part = lax.optimization_barrier((returned, back_part))
    bound = returned.transpose(1, 2, 0, 3).reshape(2, modes, channels)
    grad_mix, short_grad = over_channels(
        apply_kernel,
        [bound, residue, decay_rate, fwd_part, back_part, key_mix, value_mix, cotangent, inputs, rim],
        [],
        [shape((3, rows, channels), bf16), shape((3, taps, channels), f32)],
        [ext_rows, pltpu.VMEM((2, rows, LANES), f32)], tile, 110 * rows * channels,
    )
    next_rim = passed_along(grad_mix[:, :RIM, :], "ctx", -1)
    terms = short_grad.reshape(3 * taps, ctx_count, narrow).transpose(1, 0, 2)
    terms = lax.all_to_all(terms, "ctx", split_axis=0, concat_axis=0, tiled=True)
    next_rim, terms = lax.optimization_barrier((next_rim, terms))
    next_rim = next_rim.astype(f32)
    own_sum = jnp.sum(terms, axis=0)
    own_squares = jnp.broadcast_to(jnp.sum(own_sum * own_sum), (1, narrow))
    packed = jnp.concatenate([own_sum, own_squares], axis=0)
    packed = jnp.broadcast_to(packed[None], (ctx_count,) + packed.shape)
    packed = lax.all_to_all(packed, "ctx", split_axis=0, concat_axis=0, tiled=True)
    (grad_inputs,) = over_channels(
        spread_kernel, [grad_mix, next_rim, short_filter], [],
        [shape((3, rows, channels), bf16)], [padded_rows], tile, 42 * rows * channels,
    )
    packed, grad_inputs = lax.optimization_barrier((packed, grad_inputs))
    short_sum = packed[:, : 3 * taps].transpose(1, 0, 2).reshape(3, taps, channels)
    squares = lax.psum(jnp.sum(packed[:, 3 * taps, 0]), "tp")
    clip_limit = math.sqrt(3 * channels * lax.axis_size("tp") * taps)
    factor = jnp.minimum(1.0, clip_limit / (jnp.sqrt(squares) + 1e-06))
    return (grad_inputs, short_sum * factor)


def solution(mesh):
    return jax.shard_map(
        per_device,
        mesh=mesh,
        in_specs=(
            P(None, "ctx", "tp"),
            P("ctx", "tp"),
            P(None, None, "tp"),
            P(None, "tp"),
            P(None, "tp"),
        ),
        out_specs=(P(None, "ctx", "tp"), P(None, None, "tp")),
        check_vma=False,
    )
```

```python
import functools
import math

import jax
import jax.numpy as jnp
import numpy as np
from jax import lax
from jax.experimental import pallas as pl
from jax.experimental.pallas import tpu as pltpu
from jax.sharding import PartitionSpec as P

LANES = 128
RIM = 8
VMEM_LIMIT = 60 * 1024 * 1024


def passed_along(shard, axis, by):
    length = lax.axis_size(axis)
    pairs = [(i, i + by) for i in range(length) if 0 <= i + by < length]
    return lax.ppermute(shard, axis, pairs)


def spectral_table(rows):
    frame = 2 * rows
    freq = np.arange(rows)[:, None]
    pos = np.arange(rows)[None, :]
    angles = (freq * pos % frame) * (2.0 * math.pi / frame)
    lower = -np.sin(angles)
    lower[0] = 1.0 - 2.0 * (np.arange(rows) % 2)
    return np.concatenate([np.cos(angles), lower], axis=0).astype(np.float32)


def split_table(table):
    high = table.astype(jnp.bfloat16)
    low = (table - high.astype(np.float32)).astype(jnp.bfloat16)
    return high, low


def mm(a, b):
    return jnp.dot(a, b, preferred_element_type=jnp.float32)


def row_ids():
    return lax.broadcasted_iota(jnp.int32, (8, LANES), 0).astype(jnp.float32)


def filter_kernel(res_ref, rate_ref, high_ref, low_ref, spec_ref, taps):
    modes, width = res_ref.shape
    rows = taps.shape[0]
    ids = row_ids()

    @pl.loop(0, width // LANES)
    def _(chunk):
        lanes = pl.ds(pl.multiple_of(chunk * LANES, LANES), LANES)
        terms = []
        steps = []
        for n in range(modes):
            rate = jnp.broadcast_to(rate_ref[n : n + 1, lanes], (8, LANES))
            terms.append(res_ref[n : n + 1, lanes] * jnp.exp(-rate * ids))
            steps.append(jnp.exp(-8.0 * rate))

        def body(block, terms):
            total = list(terms)
            while len(total) > 1:
                total = [total[i] + total[i + 1] for i in range(0, len(total) - 1, 2)] + (
                    [total[-1]] if len(total) % 2 else []
                )
            taps[pl.ds(pl.multiple_of(block * 8, 8), 8), lanes] = total[0]
            return tuple(t * s for t, s in zip(terms, steps))

        lax.fori_loop(0, rows // 8, body, tuple(terms), unroll=8)

    whole = taps[...]
    main = whole.astype(jnp.bfloat16)
    rest = (whole - main.astype(jnp.float32)).astype(jnp.bfloat16)
    spec = mm(high_ref[...], main) + (mm(low_ref[...], main) + mm(high_ref[...], rest))
    index = lax.broadcasted_iota(jnp.int32, spec.shape, 0)
    edge = jnp.logical_or(index == 0, index == rows)
    spec_ref[...] = spec * jnp.where(edge, 0.5 / rows, 1.0 / rows)


def fill_extended(ext, in_ref, rim_ref, lanes):
    rows = in_ref.shape[1]
    for i in range(3):
        ext[i, 0:RIM, :] = rim_ref[i, :, lanes]
        ext[i, RIM : RIM + rows, :] = in_ref[i, :, lanes].astype(jnp.float32)


def mix_kernel(
    in_ref, rim_ref, cot_ref, short_ref, rate_ref,
    gated_ref, grad_ref, key_ref, value_ref, state_ref, ext, rowed,
):
    rows, width = cot_ref.shape
    modes = rate_ref.shape[0]
    taps = short_ref.shape[1]
    half = (taps + 1) // 2
    part = 64
    ids = row_ids()

    @pl.loop(0, width // LANES)
    def _(chunk):
        lanes = pl.ds(pl.multiple_of(chunk * LANES, LANES), LANES)
        for i in range(3):
            ext[i, 0:RIM, :] = jnp.zeros((RIM, LANES), jnp.float32)
            ext[i, RIM : 2 * RIM, :] = rim_ref[i, :, lanes]
            ext[i, 2 * RIM : 2 * RIM + rows, :] = in_ref[i, :, lanes].astype(jnp.float32)
        for first in range(0, rows, part):
            mixed = []
            for i in range(3):
                near = None
                far = None
                for m in range(half):
                    seen = ext[i, first + RIM - m : first + 2 * RIM - m + part, :]
                    term = short_ref[i, m : m + 1, lanes] * seen[RIM:]
                    near = term if near is None else near + term
                    if half + m < taps:
                        term = short_ref[i, half + m : half + m + 1, lanes] * seen
                        far = term if far is None else far + term
                mixed.append(near + pltpu.roll(far, half, 0)[RIM:])
            here = slice(first, first + part)
            gated_ref[here, lanes] = (mixed[1] * mixed[2]).astype(jnp.bfloat16)
            grad_ref[here, lanes] = (cot_ref[here, lanes].astype(jnp.float32) * mixed[0]).astype(jnp.bfloat16)
            key_ref[here, lanes] = mixed[1].astype(jnp.bfloat16)
            value_ref[here, lanes] = mixed[2].astype(jnp.bfloat16)

        steps = [
            jnp.exp(-8.0 * jnp.broadcast_to(rate_ref[n : n + 1, lanes], (8, LANES)))
            for n in range(modes)
        ]

        def body(block, carry):
            ends, starts = carry
            up = pl.multiple_of(block * 16, 16)
            down = pl.multiple_of(rows - 16 - block * 16, 16)
            ahead = gated_ref[pl.ds(up, 16), lanes].astype(jnp.float32)
            behind = grad_ref[pl.ds(down, 16), lanes].astype(jnp.float32)
            ends = [e * s + ahead[0:8] for e, s in zip(ends, steps)]
            starts = [e * s + behind[8:16] for e, s in zip(starts, steps)]
            ends = [e * s + ahead[8:16] for e, s in zip(ends, steps)]
            starts = [e * s + behind[0:8] for e, s in zip(starts, steps)]
            return tuple(ends), tuple(starts)

        zero = tuple(jnp.zeros((8, LANES), jnp.float32) for _ in range(modes))
        ends, starts = lax.fori_loop(0, rows // 16, body, (zero, zero), unroll=8)
        for n in range(modes):
            rate = jnp.broadcast_to(rate_ref[n : n + 1, lanes], (8, LANES))
            rowed[n : n + 1, :] = jnp.sum(ends[n] * jnp.exp(-rate * (7.0 - ids)), axis=0, keepdims=True)
            rowed[modes + n : modes + n + 1, :] = jnp.sum(
                starts[n] * jnp.exp(-rate * ids), axis=0, keepdims=True
            )
        state_ref[0, :, lanes] = rowed[0:modes, :].astype(jnp.bfloat16)
        state_ref[1, :, lanes] = rowed[modes : 2 * modes, :].astype(jnp.bfloat16)


def local_kernel(sign, signal_ref, spec_ref, high_ref, low_ref, hight_ref, lowt_ref, out_ref):
    rows = signal_ref.shape[0]
    real = spec_ref[0:rows, :]
    lower = spec_ref[rows : 2 * rows, :]
    first = lax.broadcasted_iota(jnp.int32, real.shape, 0) == 0
    imag = sign * jnp.where(first, 0.0, lower)
    other = jnp.where(first, lower, real)
    seen = mm(high_ref[...], signal_ref[...]) + mm(low_ref[...], signal_ref[...])
    a = seen[0:rows, :]
    b = seen[rows : 2 * rows, :]
    top = (a * real - b * imag).astype(jnp.bfloat16)
    bottom = (a * imag + b * other).astype(jnp.bfloat16)
    both = jnp.concatenate([top, bottom], axis=0)
    out_ref[...] = mm(hight_ref[...], both) + mm(lowt_ref[...], both)


def scan_kernel(states_ref, step_ref, out_ref):
    count = states_ref.shape[0]
    step = step_ref[...]
    zero = jnp.zeros(step.shape, jnp.float32)

    def up(j, carry):
        out_ref[j, 0, :, :] = carry.astype(jnp.bfloat16)
        return carry * step + states_ref[j, 0, :, :].astype(jnp.float32)

    lax.fori_loop(0, count, up, zero)

    def down(i, carry):
        j = count - 1 - i
        out_ref[j, 1, :, :] = carry.astype(jnp.bfloat16)
        return carry * step + states_ref[j, 1, :, :].astype(jnp.float32)

    lax.fori_loop(0, count, down, zero)


def apply_kernel(
    bound_ref, res_ref, rate_ref, fwd_ref, back_ref, key_ref, value_ref, cot_ref, in_ref, rim_ref,
    gm_ref, short_ref, ext, far,
):
    rows, width = cot_ref.shape
    modes = rate_ref.shape[0]
    taps = short_ref.shape[1]
    part = 32
    ids = row_ids()

    @pl.loop(0, width // LANES)
    def _(chunk):
        lanes = pl.ds(pl.multiple_of(chunk * LANES, LANES), LANES)
        fill_extended(ext, in_ref, rim_ref, lanes)
        before = bound_ref[0, :, lanes].astype(jnp.float32) * res_ref[:, lanes]
        after = bound_ref[1, :, lanes].astype(jnp.float32) * res_ref[:, lanes]
        ups = []
        downs = []
        steps = []
        for n in range(modes):
            rate = jnp.broadcast_to(rate_ref[n : n + 1, lanes], (8, LANES))
            ups.append(before[n : n + 1, :] * jnp.exp(-rate * (ids + 1.0)))
            downs.append(after[n : n + 1, :] * jnp.exp(-rate * (8.0 - ids)))
            steps.append(jnp.exp(-8.0 * rate))

        def summed(terms):
            total = list(terms)
            while len(total) > 1:
                total = [total[i] + total[i + 1] for i in range(0, len(total) - 1, 2)] + (
                    [total[-1]] if len(total) % 2 else []
                )
            return total[0]

        def body(block, carry):
            ups, downs = carry
            up = pl.ds(pl.multiple_of(block * 8, 8), 8)
            down = pl.ds(pl.multiple_of(rows - 8 - block * 8, 8), 8)
            far[0, up, :] = fwd_ref[up, lanes] + summed(ups)
            far[1, down, :] = back_ref[down, lanes] + summed(downs)
            return (
                tuple(t * s for t, s in zip(ups, steps)),
                tuple(t * s for t, s in zip(downs, steps)),
            )

        lax.fori_loop(0, rows // 8, body, (tuple(ups), tuple(downs)), unroll=8)

        sums = [[None] * taps for _ in range(3)]
        for first in range(0, rows, part):
            here = slice(first, first + part)
            mixer = far[0, here, :]
            back = far[1, here, :]
            grads = (
                cot_ref[here, lanes].astype(jnp.float32) * mixer,
                back * value_ref[here, lanes].astype(jnp.float32),
                back * key_ref[here, lanes].astype(jnp.float32),
            )
            for i in range(3):
                kept = grads[i].astype(jnp.bfloat16)
                gm_ref[i, here, lanes] = kept
                wide = kept.astype(jnp.float32)
                for j in range(taps):
                    term = wide * ext[i, first + RIM - j : first + RIM - j + part, :]
                    folded = jnp.sum(term.reshape(part // 8, 8, LANES), axis=0)
                    sums[i][j] = folded if sums[i][j] is None else sums[i][j] + folded
        for i in range(3):
            for j in range(taps):
                short_ref[i, j : j + 1, lanes] = jnp.sum(sums[i][j], axis=0, keepdims=True)


def spread_kernel(gm_ref, rim_ref, short_ref, out_ref, ext):
    rows, width = gm_ref.shape[1:]
    taps = short_ref.shape[1]
    half = (taps + 1) // 2
    part = 64

    @pl.loop(0, width // LANES)
    def _(chunk):
        lanes = pl.ds(pl.multiple_of(chunk * LANES, LANES), LANES)
        for i in range(3):
            ext[i, 0:rows, :] = gm_ref[i, :, lanes].astype(jnp.float32)
            ext[i, rows : rows + RIM, :] = rim_ref[i, :, lanes]
            ext[i, rows + RIM : rows + 2 * RIM, :] = jnp.zeros((RIM, LANES), jnp.float32)
        for first in range(0, rows, part):
            for i in range(3):
                near = None
                far = None
                for m in range(half):
                    seen = ext[i, first + m : first + m + part + RIM, :]
                    term = short_ref[i, m : m + 1, lanes] * seen[0:part]
                    near = term if near is None else near + term
                    if half + m < taps:
                        term = short_ref[i, half + m : half + m + 1, lanes] * seen
                        far = term if far is None else far + term
                total = near + pltpu.roll(far, part + RIM - half, 0)[0:part]
                out_ref[i, first : first + part, lanes] = total.astype(jnp.bfloat16)


def tiled(shape, tile):
    lead = len(shape) - 1
    return pl.BlockSpec(tuple(shape[:-1]) + (tile,), lambda c: (0,) * lead + (c,))


def fixed(shape):
    return pl.BlockSpec(tuple(shape), lambda c: (0,) * len(shape))


def over_channels(kernel, operands, tables, outs, scratch, tile, flops):
    channels = operands[0].shape[-1]
    total_bytes = sum(a.size * a.dtype.itemsize for a in operands + tables)
    total_bytes += sum(math.prod(o.shape) * o.dtype.itemsize for o in outs)
    return pl.pallas_call(
        kernel,
        grid=(channels // tile,),
        in_specs=[tiled(a.shape, tile) for a in operands] + [fixed(a.shape) for a in tables],
        out_specs=[tiled(o.shape, tile) for o in outs],
        out_shape=outs,
        scratch_shapes=scratch,
        compiler_params=pltpu.CompilerParams(vmem_limit_bytes=VMEM_LIMIT),
        cost_estimate=pl.CostEstimate(flops=flops, bytes_accessed=total_bytes, transcendentals=0),
    )(*operands, *tables)


def per_device(inputs, cotangent, short_filter, residue, decay_rate):
    rows, channels = cotangent.shape
    modes = residue.shape[0]
    taps = short_filter.shape[1]
    ctx_count = lax.axis_size("ctx")
    narrow = channels // ctx_count
    tile = math.gcd(channels, 1024)
    f32 = jnp.float32
    bf16 = jnp.bfloat16
    shape = jax.ShapeDtypeStruct
    high, low = split_table(spectral_table(rows))
    tables = [jnp.asarray(high), jnp.asarray(low)]
    turned = [jnp.asarray(np.ascontiguousarray(high.T)), jnp.asarray(np.ascontiguousarray(low.T))]
    padded_rows = pltpu.VMEM((3, rows + 2 * RIM, LANES), f32)
    ext_rows = pltpu.VMEM((3, rows + RIM, LANES), f32)

    rim = passed_along(inputs[:, rows - RIM :, :], "ctx", 1).astype(f32)
    (spec,) = over_channels(
        filter_kernel, [residue, decay_rate], tables,
        [shape((2 * rows, channels), f32)], [pltpu.VMEM((rows, tile), f32)], tile,
        6 * 2 * rows * rows * channels,
    )
    rim, spec = lax.optimization_barrier((rim, spec))
    gated, grad_mixer, key_mix, value_mix, states = over_channels(
        mix_kernel, [inputs, rim, cotangent, short_filter, decay_rate], [],
        [shape((rows, channels), bf16)] * 4 + [shape((2, modes, channels), bf16)],
        [padded_rows, pltpu.VMEM((2 * modes, LANES), f32)], tile, 110 * rows * channels,
    )
    sent = states.reshape(2, modes, ctx_count, narrow).transpose(2, 0, 1, 3)
    arrived = lax.all_to_all(sent, "ctx", split_axis=0, concat_axis=0, tiled=True)
    def local(sign, signal):
        return over_channels(
            functools.partial(local_kernel, sign), [signal, spec], tables + turned,
            [shape((rows, channels), f32)], [], tile, 8 * 2 * rows * rows * channels,
        )[0]

    fwd_part = local(1.0, gated)
    arrived, fwd_part = lax.optimization_barrier((arrived, fwd_part))
    first_chan = lax.axis_index("ctx") * narrow
    rate_part = lax.dynamic_slice_in_dim(decay_rate, first_chan, narrow, 1)
    bounds = pl.pallas_call(
        scan_kernel,
        out_shape=shape(arrived.shape, bf16),
        compiler_params=pltpu.CompilerParams(vmem_limit_bytes=VMEM_LIMIT),
    )(arrived, jnp.exp(-rate_part * rows))
    returned = lax.all_to_all(bounds, "ctx", split_axis=0, concat_axis=0, tiled=True)
    back_part = local(-1.0, grad_mixer)
    returned, back_part = lax.optimization_barrier((returned, back_part))
    bound = returned.transpose(1, 2, 0, 3).reshape(2, modes, channels)
    grad_mix, short_grad = over_channels(
        apply_kernel,
        [bound, residue, decay_rate, fwd_part, back_part, key_mix, value_mix, cotangent, inputs, rim],
        [],
        [shape((3, rows, channels), bf16), shape((3, taps, channels), f32)],
        [ext_rows, pltpu.VMEM((2, rows, LANES), f32)], tile, 110 * rows * channels,
    )
    next_rim = passed_along(grad_mix[:, :RIM, :], "ctx", -1)
    terms = short_grad.reshape(3 * taps, ctx_count, narrow).transpose(1, 0, 2)
    terms = lax.all_to_all(terms, "ctx", split_axis=0, concat_axis=0, tiled=True)
    next_rim, terms = lax.optimization_barrier((next_rim, terms))
    next_rim = next_rim.astype(f32)
    own_sum = jnp.sum(terms, axis=0)
    own_squares = jnp.broadcast_to(jnp.sum(own_sum * own_sum), (1, narrow))
    packed = jnp.concatenate([own_sum, own_squares], axis=0)
    packed = jnp.broadcast_to(packed[None], (ctx_count,) + packed.shape)
    packed = lax.all_to_all(packed, "ctx", split_axis=0, concat_axis=0, tiled=True)
    (grad_inputs,) = over_channels(
        spread_kernel, [grad_mix, next_rim, short_filter], [],
        [shape((3, rows, channels), bf16)], [padded_rows], tile, 42 * rows * channels,
    )
    packed, grad_inputs = lax.optimization_barrier((packed, grad_inputs))
    short_sum = packed[:, : 3 * taps].transpose(1, 0, 2).reshape(3, taps, channels)
    squares = lax.psum(jnp.sum(packed[:, 3 * taps, 0]), "tp")
    clip_limit = math.sqrt(3 * channels * lax.axis_size("tp") * taps)
    factor = jnp.minimum(1.0, clip_limit / (jnp.sqrt(squares) + 1e-06))
    return (grad_inputs, short_sum * factor)


def solution(mesh):
    return jax.shard_map(
        per_device,
        mesh=mesh,
        in_specs=(
            P(None, "ctx", "tp"),
            P("ctx", "tp"),
            P(None, None, "tp"),
            P(None, "tp"),
            P(None, "tp"),
        ),
        out_specs=(P(None, "ctx", "tp"), P(None, None, "tp")),
        check_vma=False,
    )
```
